32 devices in a mesh: req: 8 (over z, y), tp: 4 (over x, core).
Axes of the slice: x: 2, y: 2, z: 4, core: 2. Of those that a mesh axis runs over, the one named last changes fastest.
Arguments:
- ssm_input: bfloat16 [8, 512, 8192], P('req', 'tp'), may hold values from -6 to 6
- ssm_gate: bfloat16 [8, 512, 8192], P('req', 'tp'), may hold values from -6 to 6
- state_proj: bfloat16 [8, 512, 4096], P('req', 'tp'), may hold values from -1.796875 to 1.796875
- step_raw: bfloat16 [8, 512, 128], P('req', 'tp'), may hold values from -3 to 3
- queries: bfloat16 [8, 512, 4096], P('req', 'tp'), may hold values from -5 to 5
- fresh_kv: bfloat16 [8, 512, 2048], P('req', 'tp'), may hold values from -6 to 6
- block_pool: bfloat16 [32, 64, 8, 256], P('req', None, 'tp'), may hold values from -5 to 5
- state_pool: bfloat16 [8, 128, 64, 256], P('req', 'tp'), may hold values from -16 to 16
- decay_log: float32 [128], P('tp'), may hold values from -10 to -1
- step_bias: float32 [128], P('tp'), may hold values from -1 to 0
- skip_gain: float32 [128], P('tp'), may hold values from 1 to 3
- norm_gain: float32 [8192], P('tp'), may hold values from 0.5 to 1.5
- block_owner: int32 [8, 64], replicated, may hold values from 0 to 7, as said below
- block_slot: int32 [8, 64], replicated, may hold values from 0 to 3, as said below
- block_count: int32 [8], replicated, may hold values from 32 to 64, as said below
- state_entry: int32 [8], replicated, may hold values from 0 to 7
- suffix_len: int32 [8], replicated, may hold values from 128 to 512, as said below
Outputs:
- ssm_out: bfloat16 [8, 512, 8192], P('req', 'tp')
- attn_out: bfloat16 [8, 512, 4096], P('req', 'tp')
The draws below stay inside these ranges and needn't reach their ends.
Inputs may be any that keep to these rules, and one draw needn't show every extreme that they name: `block_owner`: among the first block_count[r] entries of a request no owner appears more than 8 times; in every draw one request has 64 entries in use and takes exactly 8 from every owner. The owner at entry j is named again at entry j + 8. Requests 4k to 4k + 3 name the same owners at every entry. `block_slot`: requests 4k to 4k + 3 name the same blocks in their first 32 entries. `block_count`: some request has 64 in every draw. `suffix_len`: some request has 512 in every draw.
All inputs are finite; a program needn't handle non-finite values.
Results may differ from the reference program's by a relative error of at most 0.0048.
Values may be sent and summed in bfloat16 or wider, within the bound.
No kernel may reach another device: no remote copies, remote signals or barrier semaphores. Data moves between devices by JAX's collectives and lax.ppermute only.
A program may use at most 128 MiB of HBM per device.

```python
import jax
import jax.numpy as jnp
from jax import lax

MHEADS = 128
HEAD_DIM = 64
STATE = 256
GROUPS = 8
QHEADS = 32
KVHEADS = 8
ATT_DIM = 128
SPAN = 256
BLOCK = 64
SUFFIX = 512
MAXBLK = 64
POOL_DEV = 4
REQS = 8
ENTRIES = 8
POOL = 32


def block_tables(key):
    key = jax.random.fold_in(key, 5)
    key_perm, key_shared, key_own = jax.random.split(key, 3)
    group_total = (REQS + 3) // 4
    perm_keys = jax.random.split(key_perm, group_total)
    orders = jax.vmap(lambda one_key: jax.random.permutation(one_key, REQS))(perm_keys)
    request_index = jnp.arange(REQS)[:, None]
    entry_index = jnp.arange(MAXBLK)[None, :]
    owners = orders[request_index // 4, entry_index % REQS]
    shared = jax.random.randint(key_shared, (group_total, MAXBLK), 0, POOL_DEV)
    own_slots = jax.random.randint(key_own, (REQS, MAXBLK), 0, POOL_DEV)
    slots = jnp.where(entry_index < MAXBLK // 2, shared[request_index // 4, entry_index], own_slots)
    return (owners.astype(jnp.int32), slots.astype(jnp.int32))


def draw_block_owner(key, part):
    return block_tables(key)[0]


def draw_block_slot(key, part):
    return block_tables(key)[1]


def draw_block_count(key, part):
    key = jax.random.fold_in(key, 21)
    key_vals, key_pick = jax.random.split(key)
    counts = jax.random.randint(key_vals, (REQS,), MAXBLK // 2, MAXBLK + 1)
    chosen = jax.random.randint(key_pick, (), 0, REQS)
    return jnp.where(jnp.arange(REQS) == chosen, MAXBLK, counts).astype(jnp.int32)


def draw_suffix_len(key, part):
    key = jax.random.fold_in(key, 23)
    key_vals, key_pick = jax.random.split(key)
    lengths = jax.random.randint(key_vals, (REQS,), SUFFIX // 4, SUFFIX + 1)
    chosen = jax.random.randint(key_pick, (), 0, REQS)
    return jnp.where(jnp.arange(REQS) == chosen, SUFFIX, lengths).astype(jnp.int32)


def draw_decay_log(key, part):
    key = jax.random.fold_in(key, 13)
    key_perm, key_unif = jax.random.split(key)
    ranks = jax.random.permutation(key_perm, MHEADS)
    slow_total = MHEADS // 2
    unit = jax.random.uniform(key_unif, (MHEADS,), jnp.float32, 0.0, 1.0)
    slow_rate = 0.5 / SUFFIX * jnp.exp(unit * 1.8)
    fast_rate = 0.05 * jnp.exp(unit * 1.1)
    rates = jnp.where(ranks < slow_total, slow_rate, fast_rate)
    return jnp.log(rates).astype(jnp.float32)


def draw_queries(key, part):
    key = jax.random.fold_in(key, 11)
    shape = (REQS, SUFFIX, QHEADS * ATT_DIM)
    values = jnp.clip(jax.random.normal(key, shape, jnp.float32), -5.0, 5.0)
    return values.astype(jnp.bfloat16)


def draw_block_pool(key, part):
    key = jax.random.fold_in(key, 17)
    shape = (POOL, BLOCK, KVHEADS, 2 * ATT_DIM)
    values = jnp.clip(jax.random.normal(key, shape, jnp.float32), -5.0, 5.0)
    return values.astype(jnp.bfloat16)


def set_ends(result, own_key, low, top_value):
    dims = result.shape
    place = [jax.random.randint(jax.random.fold_in(own_key, axis), (), 0, dims[axis]) for axis in range(len(dims))]
    result = result.at[tuple(place)].set(low)
    longest = dims.index(max(dims))
    place[longest] = (place[longest] + 1) % dims[longest]
    return result.at[tuple(place)].set(top_value)


def block_scale(key, dims, shards, least, high):
    factor_of = 1.0
    for dim, parts in shards:
        steps = jax.random.uniform(jax.random.fold_in(jax.random.fold_in(key, 6), dim), (parts,), jnp.float32, least / len(shards), high / len(shards))
        factor_of = factor_of * jnp.repeat(jnp.exp(steps), dims[dim] // parts).reshape((-1,) + (1,) * (len(dims) - 1 - dim))
    return factor_of


def scatter_about(stream_key, dims, deviation, reach, cuts=(), kind=jnp.bfloat16):
    values = jax.random.normal(stream_key, dims, jnp.float32) * deviation
    if len(cuts) > 0:
        values = block_scale(stream_key, dims, cuts, -0.22, 0.18) * values
    return jnp.clip(values, min=-reach, max=reach).astype(kind)


def setup_inputs(seed: int = 0) -> dict:
    splits = jax.random.split(jax.random.key(seed), 18)
    return {
        "ssm_input": scatter_about(splits[0], (REQS, SUFFIX, MHEADS * HEAD_DIM), 1.0, 6.0, ((0, 8), (1, 4))),
        "ssm_gate": scatter_about(splits[1], (REQS, SUFFIX, MHEADS * HEAD_DIM), 1.0, 6.0, ((0, 8), (1, 4))),
        "state_proj": scatter_about(splits[2], (REQS, SUFFIX, 2 * GROUPS * STATE), 0.3, 1.796875, ((0, 8), (1, 4))),
        "step_raw": scatter_about(splits[3], (REQS, SUFFIX, MHEADS), 0.5, 3.0, ((0, 8), (1, 4))),
        "queries": draw_queries(jax.random.fold_in(splits[17], 71), 0),
        "fresh_kv": scatter_about(splits[5], (REQS, SUFFIX, 2 * KVHEADS * ATT_DIM), 1.0, 6.0, ((0, 8), (1, 4))),
        "block_pool": draw_block_pool(jax.random.fold_in(splits[17], 71), 0),
        "state_pool": scatter_about(splits[7], (ENTRIES, MHEADS, HEAD_DIM, STATE), 4.0, 16.0, ((0, 8), (1, 4))),
        "decay_log": draw_decay_log(jax.random.fold_in(splits[17], 71), 0),
        "step_bias": jnp.clip(-1.0 + 1.0 * jax.random.uniform(splits[9], (MHEADS,), jnp.float32) ** block_scale(splits[9], (MHEADS,), ((0, 4),), -0.2, 0.2), -1.0, 0.0),
        "skip_gain": jnp.clip(1.0 + 2.0 * jax.random.uniform(splits[10], (MHEADS,), jnp.float32) ** block_scale(splits[10], (MHEADS,), ((0, 4),), -0.2, 0.2), 1.0, 3.0),
        "norm_gain": jnp.clip(1.0 + 0.1 * jax.random.normal(splits[11], (MHEADS * HEAD_DIM,), jnp.float32), 0.5, 1.5),
        "block_owner": draw_block_owner(jax.random.fold_in(splits[17], 71), 0),
        "block_slot": draw_block_slot(jax.random.fold_in(splits[17], 71), 0),
        "block_count": draw_block_count(jax.random.fold_in(splits[17], 71), 0),
        "state_entry": set_ends(jax.random.randint(splits[15], (REQS,), 0, ENTRIES), jax.random.fold_in(splits[15], 1), 0, ENTRIES - 1).astype(jnp.int32),
        "suffix_len": draw_suffix_len(jax.random.fold_in(splits[17], 71), 0),
    }


HIGH = lax.Precision.HIGHEST

def rounded(value):
    return lax.optimization_barrier(value.astype(jnp.bfloat16)).astype(jnp.float32)

def scan_heads(ssm_rows, gate_rows, proj_rows, step_rows, initial, decay_log, step_bias, skip_gain, norm_gain, live_len, group_count):
    length_all, width = ssm_rows.shape
    head_count = step_rows.shape[1]
    head_size = width // head_count
    per_group = head_count // group_count
    state_size = proj_rows.shape[1] // (2 * group_count)
    block_count = length_all // SPAN
    inputs = ssm_rows.astype(jnp.float32).reshape(block_count, SPAN, group_count, per_group, head_size)
    proj_four = proj_rows.astype(jnp.float32).reshape(block_count, SPAN, group_count, 2, state_size)
    in_proj = proj_four[:, :, :, 0]
    out_proj = proj_four[:, :, :, 1]
    step_size = jax.nn.softplus(step_rows.astype(jnp.float32) + step_bias[None, :])
    step_size = step_size.reshape(block_count, SPAN, group_count, per_group)
    rates = jnp.exp(decay_log).reshape(group_count, per_group)
    skip_heads = skip_gain.reshape(group_count, per_group)
    lower = jnp.arange(SPAN)[:, None] >= jnp.arange(SPAN)[None, :]

    def advance(state, block_in):
        block_x, block_b, block_c, block_dt = block_in
        cumul = jnp.cumsum(-rates[None] * block_dt, axis=0)
        inner = jnp.einsum('tgn,ugn->tug', block_c, block_b, precision=HIGH)
        spread = cumul[:, None] - cumul[None, :]
        decay = jnp.exp(jnp.where(lower[:, :, None, None], spread, -jnp.inf))
        mixing = rounded(decay * inner[:, :, :, None] * block_dt[None])
        output = jnp.einsum('tugh,ughp->tghp', mixing, block_x, precision=HIGH)
        state_in = rounded(state)
        carried = jnp.einsum('tgn,ghpn->tghp', block_c, state_in, precision=HIGH)
        output = output + jnp.exp(cumul)[..., None] * carried
        output = output + skip_heads[None, :, :, None] * block_x
        tail_weight = jnp.exp(cumul[-1][None] - cumul) * block_dt
        tail_terms = rounded(tail_weight[..., None] * block_x)
        state = jnp.exp(cumul[-1])[:, :, None, None] * state + jnp.einsum('ughp,ugn->ghpn', tail_terms, block_b, precision=HIGH)
        return (state, output)
    start_state = initial.reshape(group_count, per_group, head_size, state_size)
    final_state, outputs = lax.scan(advance, start_state, (inputs, in_proj, out_proj, step_size))
    outputs = outputs.reshape(length_all, group_count, per_group * head_size)
    gated = outputs * jax.nn.silu(gate_rows.astype(jnp.float32)).reshape(length_all, group_count, per_group * head_size)
    mean_sq = lax.optimization_barrier(jnp.mean(gated * gated, axis=-1, keepdims=True))
    normed = gated * lax.rsqrt(mean_sq + 1e-05) * norm_gain.reshape(group_count, per_group * head_size)
    normed = normed.reshape(length_all, width)
    alive = jnp.arange(length_all) < live_len
    return jnp.where(alive[:, None], normed, 0.0).astype(jnp.bfloat16)

def attend(query_rows, key_rows, value_rows, prefix_live, live_len):
    length_all, kv_count, repeat, head_size = query_rows.shape
    key_total = key_rows.shape[0]
    prefix_rows = key_total - length_all
    rows_block = min(256, length_all)
    inv_root = 1.0 / head_size ** 0.5
    key_index = jnp.arange(key_total)
    keys_wide = key_rows.astype(jnp.float32)
    values_wide = value_rows.astype(jnp.float32)

    def one_block(offset):
        block_q = lax.dynamic_slice_in_dim(query_rows, offset, rows_block, 0).astype(jnp.float32)
        scores = jnp.einsum('qcrd,kcd->crqk', block_q, keys_wide) * inv_root
        query_index = offset + jnp.arange(rows_block)
        allowed = jnp.where(key_index[None, :] < prefix_rows, key_index[None, :] < prefix_live, key_index[None, :] - prefix_rows <= query_index[:, None])
        scores = jnp.where(allowed[None, None], scores, -jnp.inf)
        row_max = lax.optimization_barrier(jnp.max(scores, axis=-1, keepdims=True))
        expon = jnp.exp(scores - row_max)
        totals = lax.optimization_barrier(jnp.sum(expon, axis=-1))
        weights = expon.astype(jnp.bfloat16).astype(jnp.float32)
        mixed = jnp.einsum('crqk,kcd->qcrd', weights, values_wide)
        mixed = mixed / jnp.transpose(totals, (2, 0, 1))[..., None]
        mixed = jnp.where((query_index < live_len)[:, None, None, None], mixed, 0.0)
        return mixed.astype(jnp.bfloat16)
    outputs = lax.map(one_block, jnp.arange(length_all // rows_block, dtype=jnp.int32) * rows_block)
    return outputs.reshape(length_all, kv_count * repeat * head_size)

def reference(ssm_input, ssm_gate, state_proj, step_raw, queries, fresh_kv, block_pool, state_pool, decay_log, step_bias, skip_gain, norm_gain, block_owner, block_slot, block_count, state_entry, suffix_len):

    def one_request(request):
        initial = state_pool[state_entry[request]].astype(jnp.float32)
        mamba = scan_heads(ssm_input[request], ssm_gate[request], state_proj[request], step_raw[request], initial, decay_log, step_bias, skip_gain, norm_gain, suffix_len[request], GROUPS)
        block_ids = (block_owner[request] * POOL_DEV + block_slot[request]).astype(jnp.int32)
        cached = block_pool[block_ids].reshape(MAXBLK * BLOCK, KVHEADS, 2 * ATT_DIM)
        newest = fresh_kv[request].reshape(SUFFIX, KVHEADS, 2 * ATT_DIM)
        joined = jnp.concatenate([cached, newest], axis=0)
        query_rows = queries[request].reshape(SUFFIX, KVHEADS, QHEADS // KVHEADS, ATT_DIM)
        attention = attend(query_rows, joined[..., :ATT_DIM], joined[..., ATT_DIM:], block_count[request] * BLOCK, suffix_len[request])
        return (mamba, attention)
    ssm_out, attn_out = lax.map(one_request, jnp.arange(REQS, dtype=jnp.int32))
    return (ssm_out, attn_out)
```

```python
import functools
import math

import jax
import jax.numpy as jnp
from jax import lax
from jax.experimental import pallas as pl
from jax.experimental.pallas import tpu as pltpu
from jax.sharding import PartitionSpec as P

STATE = 256
SPAN = 256
TILE = 256
VMEM = 60 * 1024 * 1024
SMALL = 8 * 1024 * 1024


def cost(microseconds=0.0):
    return pl.CostEstimate(
        flops=1024 + int(microseconds * 1.15e9), bytes_accessed=1024, transcendentals=0
    )


def params(limit=VMEM):
    return pltpu.CompilerParams(vmem_limit_bytes=limit)


def dot_nt(left, right):
    return lax.dot_general(left, right, (((1,), (1,)), ((), ())), preferred_element_type=jnp.float32)


def dot_tn(left, right):
    return lax.dot_general(left, right, (((0,), (0,)), ((), ())), preferred_element_type=jnp.float32)


def pack(parts, pieces, gain):
    rows = pieces[0][0].shape[0]
    widths = [width for _, width, _ in pieces]
    gain_rows, lanes = gain.shape
    total = sum(widths) + lanes

    def body(*refs):
        *piece_refs, gain_ref, out_ref = refs
        at = 0
        for ref, width in zip(piece_refs, widths):
            out_ref[:, at : at + width] = ref[...]
            at += width
        terms, rest = [], gain_ref[...]
        for _ in range(3):
            terms.append(rest.astype(jnp.bfloat16).astype(jnp.float32))
            rest = rest - terms[-1]
        terms.append(jnp.zeros((rows - 3 * gain_rows, lanes), jnp.float32))
        out_ref[:, at:] = jnp.concatenate(terms, axis=0).astype(jnp.bfloat16)

    specs = [
        pl.BlockSpec((rows, width), functools.partial(lambda place, p: (0, place(p)), place))
        for _, width, place in pieces
    ]
    return pl.pallas_call(
        body,
        grid=(parts,),
        in_specs=specs + [pl.BlockSpec(gain.shape, lambda p: (0, 0))],
        out_specs=pl.BlockSpec((None, rows, total), lambda p: (p, 0, 0)),
        out_shape=jax.ShapeDtypeStruct((parts, rows, total), jnp.bfloat16),
        compiler_params=params(),
        cost_estimate=cost(),
    )(*[array for array, _, _ in pieces], gain)


def spread(packed):
    return lax.all_to_all(packed, "tp", split_axis=0, concat_axis=0, tiled=True)


def swap(value, axis, mask):
    count = lax.axis_size(axis)
    return lax.ppermute(value, axis, [(i, i ^ mask) for i in range(count)])


def exchange(buffers):
    return [buffers[0]] + [swap(buffers[k], "tp", k) for k in range(1, len(buffers))]


def after(value, *others):
    return lax.optimization_barrier((value, *others))[0]


def join_body(one_ref, two_ref, out_ref):
    half = one_ref.shape[0]
    out_ref[:half] = one_ref[...]
    out_ref[half:] = two_ref[...]


def join(one, two):
    shape = (one.shape[0] + two.shape[0],) + one.shape[1:]
    return pl.pallas_call(
        join_body,
        out_shape=jax.ShapeDtypeStruct(shape, one.dtype),
        compiler_params=params(SMALL),
        cost_estimate=cost(15),
    )(one, two)


def block_places(targets, used_entries, pool_total):
    blocks = jnp.arange(pool_total, dtype=jnp.int32)
    live = jnp.arange(targets.shape[0]) < used_entries
    named = (targets[:, None] == blocks[None, :]) & live[:, None]
    often = jnp.sum(named.astype(jnp.int32), axis=0)
    used = often > 0
    place = jnp.sum((used[None, :] & (blocks[None, :] < blocks[:, None])).astype(jnp.int32), axis=1)
    total = jnp.sum(used.astype(jnp.int32))
    return often, place.astype(jnp.int32), total.astype(jnp.int32)


def attention_body(parts, pool_offsets, listed, size, where_ref, often_ref, place_ref, q_ref, fresh_ref, *refs):
    pool_refs = refs[: len(pool_offsets)]
    out_ref, key_ref, value_ref = refs[len(pool_offsets) :]
    rows = q_ref.shape[1]
    repeat = q_ref.shape[2] // size
    fresh, block = fresh_ref.shape[0], pool_refs[0].shape[1]
    prefix = listed * block
    scale = math.log2(math.e) / math.sqrt(size)
    request, total = where_ref[0], where_ref[1]

    for pool_ref, offsets in zip(pool_refs, pool_offsets):
        slots = pool_ref.shape[0] // len(offsets)
        for index, offset in enumerate(offsets):
            for slot in range(slots):
                number = (request ^ offset) * slots + slot
                times = often_ref[number]

                @pl.when(times > 0)
                def _(pool_ref=pool_ref, held=index * slots + slot, number=number, times=times):
                    at = pl.ds(pl.multiple_of(place_ref[number] * block, block), block)
                    pair = pool_ref[held]
                    often = times.astype(jnp.float32)
                    key_ref[at, :] = pair[:, :size]
                    value_ref[at, :size] = (pair[:, size:].astype(jnp.float32) * often).astype(jnp.bfloat16)
                    value_ref[at, size:] = jnp.full((block, size), often, jnp.float32).astype(jnp.bfloat16)

    def fill(step, carry):
        at = pl.ds(pl.multiple_of(step * block, block), block)
        key_ref[at, :] = key_ref[:block, :]
        value_ref[at, :] = jnp.zeros((block, 2 * size), jnp.bfloat16)
        return carry

    lax.fori_loop(total, listed, fill, 0)
    key_ref[prefix:, :] = fresh_ref[:, :size]
    value_ref[prefix:, :size] = fresh_ref[:, size:]
    value_ref[prefix:, size:] = jnp.ones((fresh, size), jnp.bfloat16)

    query_at = lax.broadcasted_iota(jnp.int32, (repeat, rows, rows), 1).reshape(repeat * rows, rows)
    below = lax.broadcasted_iota(jnp.int32, (repeat * rows, rows), 1) <= query_at

    def scores(k):
        queries = jnp.concatenate(
            [q_ref[k, :, head * size : (head + 1) * size] for head in range(repeat)], axis=0
        )
        whole = prefix + k * rows
        return dot_nt(queries, key_ref[:whole, :]), dot_nt(queries, key_ref[whole : whole + rows, :])

    following = scores(0)
    for k in range(parts):
        seen, edge = following
        if k + 1 < parts:
            following = scores(k + 1)
        whole = prefix + k * rows
        edge = jnp.where(below, edge, -jnp.inf)
        top = jnp.maximum(
            jnp.max(seen, axis=1, keepdims=True), jnp.max(edge, axis=1, keepdims=True)
        )
        seen = jnp.exp2((seen - top) * scale).astype(jnp.bfloat16)
        edge = jnp.exp2((edge - top) * scale).astype(jnp.bfloat16)
        mixed = jnp.dot(seen, value_ref[:whole, :], preferred_element_type=jnp.float32)
        mixed += jnp.dot(edge, value_ref[whole : whole + rows, :], preferred_element_type=jnp.float32)
        result = (mixed[:, :size] / mixed[:, size:]).astype(jnp.bfloat16)
        for head in range(repeat):
            out_ref[k, :, head * size : (head + 1) * size] = result[head * rows : (head + 1) * rows]


def attention(first, pools, where, often, place, listed, q_column, q_width):
    parts, rows, _ = first.shape
    _, kv_local, block, pair = pools[0][0].shape
    size = pair // 2
    per_kv = q_width // kv_local
    keys = listed * block + rows * parts
    specs = [
        pl.BlockSpec((parts, rows, per_kv), lambda c, *_: (0, 0, q_column // per_kv + c)),
        pl.BlockSpec((rows * parts, pair), lambda c, *_: (0, (q_column + q_width) // pair + c)),
    ]
    specs += [
        pl.BlockSpec((array.shape[0], None, block, pair), lambda c, *_: (0, c, 0, 0)) for array, _ in pools
    ]
    return pl.pallas_call(
        functools.partial(attention_body, parts, [offsets for _, offsets in pools], listed, size),
        grid_spec=pltpu.PrefetchScalarGridSpec(
            num_scalar_prefetch=3,
            grid=(kv_local,),
            in_specs=specs,
            out_specs=pl.BlockSpec((parts, rows, per_kv), lambda c, *_: (0, 0, c)),
            scratch_shapes=[
                pltpu.VMEM((keys, size), jnp.bfloat16),
                pltpu.VMEM((keys, 2 * size), jnp.bfloat16),
            ],
        ),
        out_shape=jax.ShapeDtypeStruct((parts, rows, q_width), jnp.bfloat16),
        compiler_params=params(),
        cost_estimate=cost(16),
    )(
        where,
        often,
        place,
        first,
        first.reshape(parts * rows, first.shape[2]),
        *[array for array, _ in pools],
    )


def scan_body(parts, sources, heads, group, where_ref, x_ref, proj_ref, raw_ref, head_ref, skip_ref, *refs):
    state_refs = refs[:sources]
    out_refs = refs[sources:-4]
    y_ref, state_ref, next_ref, sem = refs[-4:]
    share = where_ref[0]
    shift = where_ref[1]
    source = where_ref[2]
    rows, width = x_ref.shape
    for index in range(sources):

        @pl.when(source == index)
        def _(index=index):
            pltpu.make_async_copy(rows_of(state_refs[index], group, width), state_ref, sem).start()

    channels = width // heads
    lane = lax.broadcasted_iota(jnp.int32, (1, 2 * channels), 1)
    first_lanes = lane < channels
    row_at = lax.broadcasted_iota(jnp.int32, (2 * channels, 1), 0)
    first_rows = row_at < channels
    lower = lax.broadcasted_iota(jnp.int32, (SPAN, SPAN), 1) <= lax.broadcasted_iota(
        jnp.int32, (SPAN, SPAN), 0
    )
    base = math.log2(math.e)
    ones = jnp.where(lower, 1.0, 0.0)
    raw = pltpu.roll(raw_ref[...].astype(jnp.float32), shift, 1) + head_ref[1:2, :]
    step = jnp.maximum(raw, 0.0) + jnp.log1p(jnp.exp(-jnp.abs(raw)))
    rates = jnp.exp(head_ref[0:1, :])
    for start in range(0, rows, SPAN):
        at = slice(start, start + SPAN)
        last_block = start + SPAN >= rows
        step_block = step[at, :]
        cumul = jnp.dot(
            ones,
            -rates * step_block,
            precision=lax.Precision.HIGHEST,
            preferred_element_type=jnp.float32,
        )
        ahead = base * cumul
        back = jnp.transpose(base * (jnp.log(step_block) - cumul))
        grown = jnp.exp(cumul)
        final = cumul[SPAN - 1 : SPAN, :]
        tail = jnp.exp(final - cumul) * step_block
        kept = jnp.exp(final)
        b_block = proj_ref[at, :STATE]
        c_block = proj_ref[at, STATE:]
        inner = dot_nt(c_block, b_block)
        if start == 0:
            pltpu.make_async_copy(rows_of(state_refs[0], group, width), state_ref, sem).wait()
        state = state_ref if start == 0 else next_ref
        carried = dot_nt(c_block, state[...])
        for pair in range(heads // 2):
            cols = slice(pair * 2 * channels, (pair + 1) * 2 * channels)
            one, two = 2 * pair, 2 * pair + 1
            x_pair = x_ref[at, cols]
            mixings = []
            for head in (one, two):
                spread_at = ahead[:, head : head + 1] + back[head : head + 1, :]
                decay = jnp.exp2(jnp.where(lower, spread_at, -jnp.inf))
                mixings.append((decay * inner).astype(jnp.bfloat16))
            nothing = jnp.zeros_like(x_pair)
            output = jnp.dot(
                mixings[0], jnp.where(first_lanes, x_pair, nothing), preferred_element_type=jnp.float32
            )
            output += jnp.dot(
                mixings[1], jnp.where(first_lanes, nothing, x_pair), preferred_element_type=jnp.float32
            )
            x_wide = x_pair.astype(jnp.float32)
            factor = jnp.where(first_lanes, grown[:, one : one + 1], grown[:, two : two + 1])
            output += factor * carried[:, cols] + skip_ref[:, cols] * x_wide
            y_ref[at, cols] = output.astype(jnp.bfloat16)
            if not last_block:
                weight = jnp.where(first_lanes, tail[:, one : one + 1], tail[:, two : two + 1])
                terms = (weight * x_wide).astype(jnp.bfloat16)
                keep = jnp.where(first_rows, kept[:, one : one + 1], kept[:, two : two + 1])
                moved = keep * state[cols, :].astype(jnp.float32) + dot_tn(terms, b_block)
                next_ref[cols, :] = moved.astype(jnp.bfloat16)
    part_rows = rows // parts
    for k in range(parts):
        at = pl.ds(pl.multiple_of((share ^ k) * part_rows, part_rows), part_rows)
        out_refs[k][...] = y_ref[at, :]


def scan_group(joined, step_column, states, where, head_rows, skip_row, heads, group, local_groups):
    parts, part_rows, _ = joined.shape
    sources = len(states)
    rows = part_rows * parts
    width = skip_row.shape[1]
    step_width = head_rows.shape[1]
    proj_width = 2 * STATE
    specs = [
        pl.BlockSpec((rows, width), lambda i, *_: (0, group)),
        pl.BlockSpec((rows, proj_width), lambda i, *_: (0, local_groups * width // proj_width + group)),
        pl.BlockSpec((rows, step_width), lambda i, *_: (0, step_column // step_width)),
        pl.BlockSpec((8, step_width), lambda i, *_: (0, 0)),
        pl.BlockSpec((1, width), lambda i, *_: (0, 0)),
    ]
    specs += [pl.BlockSpec(memory_space=pl.ANY)] * sources
    flat = joined.reshape(rows, joined.shape[2])
    return pl.pallas_call(
        functools.partial(scan_body, parts, sources, heads, group),
        grid_spec=pltpu.PrefetchScalarGridSpec(
            num_scalar_prefetch=1,
            grid=(1,),
            in_specs=specs,
            out_specs=[pl.BlockSpec((part_rows, width), lambda i, *_: (0, 0))] * parts,
            scratch_shapes=[
                pltpu.VMEM((rows, width), jnp.bfloat16),
                pltpu.VMEM((width, STATE), jnp.bfloat16),
                pltpu.VMEM((width, STATE), jnp.bfloat16),
                pltpu.SemaphoreType.DMA,
            ],
        ),
        out_shape=[jax.ShapeDtypeStruct((part_rows, width), jnp.bfloat16)] * parts,
        compiler_params=params(),
        cost_estimate=cost(8),
    )(where, flat, flat, flat, head_rows, skip_row, *states)


def rows_of(ref, group, size):
    return ref if ref.shape[0] == size else ref.at[group * size : (group + 1) * size]


def choose_body(sources, group, index_ref, *refs):
    out_ref, sem = refs[sources:]
    size = out_ref.shape[0]
    for index in range(sources):

        @pl.when(index_ref[0] == index)
        def _(index=index):
            pltpu.make_async_copy(rows_of(refs[index], group, size), out_ref, sem).start()

    pltpu.make_async_copy(rows_of(refs[0], group, size), out_ref, sem).wait()


def choose(index, arrays, group, size):
    return pl.pallas_call(
        functools.partial(choose_body, len(arrays), group),
        grid_spec=pltpu.PrefetchScalarGridSpec(
            num_scalar_prefetch=1,
            grid=(1,),
            in_specs=[pl.BlockSpec(memory_space=pl.ANY)] * len(arrays),
            out_specs=pl.BlockSpec((size, STATE), lambda i, *_: (0, 0)),
            scratch_shapes=[pltpu.SemaphoreType.DMA],
        ),
        out_shape=jax.ShapeDtypeStruct((size, STATE), jnp.bfloat16),
        compiler_params=params(SMALL),
        cost_estimate=cost(),
    )(index, *arrays)


def bit_order(count, group):
    bits = count.bit_length() - 1
    if group % 2 == 0:
        return [bits - 1] + list(range(bits - 1))
    return [bits - 2] + list(range(bits - 2)) + [bits - 1]


def slot_of(distance, offsets):
    return sum(jnp.where(distance == offset, i, 0) for i, offset in enumerate(offsets))


def fetch_state(own, far, far_mask, entries, order, gate, late_gate, group):
    count = lax.axis_size("req")
    size = own.shape[0]
    offsets, held = [0], [own]
    for step, bit in enumerate(order[:-1]):
        mask = 1 << bit
        moved = []
        for offset, value in zip(offsets, held):
            if offset == 0 and mask == far_mask:
                moved.append(far)
            else:
                moved.append(swap(after(value, *(late_gate if step else gate)), "req", mask))
        held = held + moved
        offsets = offsets + [offset ^ mask for offset in offsets]
    last = 1 << order[-1]
    every = jnp.arange(count, dtype=jnp.int32)
    bits = len(order)
    flipped = jnp.flip(entries.reshape((2,) * bits), bits - 1 - order[-1]).reshape(count)
    distance = entries ^ every
    source = jnp.where((distance & last) == 0, slot_of(distance, offsets), len(held))
    choices = jnp.stack([slot_of(flipped ^ every, offsets), source]).astype(jnp.int32)
    mine = lax.dynamic_slice_in_dim(choices, lax.axis_index("req"), 1, axis=1)[:, 0]
    begun = choose(mine[0:1], held, group, size)
    return mine[1], held + [swap(begun, "req", last)], begun


def norm_body(parts, group, local_groups, where_ref, *refs):
    y_refs = refs[:parts]
    gate_refs = refs[parts : 2 * parts]
    gain_refs = refs[2 * parts : 3 * parts]
    out_ref, done_ref, sem = refs[-3:]
    share, live = where_ref[0], where_ref[1]
    number, steps = pl.program_id(0), pl.num_programs(0)
    rows, width = y_refs[0].shape
    row_at = lax.broadcasted_iota(jnp.int32, (rows, 1), 0) + number * rows
    lanes = gain_refs[0].shape[1]
    chunks = width // lanes
    third = chunks * local_groups

    def placing(step, k):
        column = pl.multiple_of(((share ^ k) * local_groups + group) * width, width)
        at = pl.ds(pl.multiple_of(step * rows, rows), rows)
        return pltpu.make_async_copy(done_ref.at[step, k], out_ref.at[at, pl.ds(column, width)], sem.at[step, k])

    for k in range(parts):
        gate = gate_refs[k][...].astype(jnp.float32)
        gated = y_refs[k][...].astype(jnp.float32) * gate * (0.5 + 0.5 * jnp.tanh(0.5 * gate))
        mean_sq = jnp.mean(gated * gated, axis=1, keepdims=True)
        normed = gated * jnp.where(row_at < live, lax.rsqrt(mean_sq + 1e-05), 0.0)
        gains = gain_refs[k][...].astype(jnp.float32)
        first = group * chunks
        gain = sum(gains[first + i * third : first + i * third + chunks] for i in range(3))
        for chunk in range(chunks):
            cols = slice(chunk * lanes, (chunk + 1) * lanes)
            done_ref[number, k, :, cols] = (normed[:, cols] * gain[chunk : chunk + 1, :]).astype(jnp.bfloat16)
        placing(number, k).start()

    @pl.when(number == steps - 1)
    def _():
        for step in range(done_ref.shape[0]):
            for k in range(parts):
                placing(step, k).wait()


def norm_group(returned, gate, joined, where, group, local_groups, earlier):
    parts = joined.shape[0]
    rows, width = returned[0].shape[-2:]
    lanes, steps = 128, 2
    step = rows // steps
    specs = [pl.BlockSpec((step, width), lambda i, *_: (i, 0))] * parts
    specs += [
        pl.BlockSpec((step, width), functools.partial(lambda k, i, at: (i, (at[0] ^ k) * local_groups + group), k))
        for k in range(parts)
    ]
    specs += [
        pl.BlockSpec(
            (None, rows, lanes),
            functools.partial(lambda k, i, at: (at[0] ^ k, 0, joined.shape[2] // lanes - 1), k),
        )
        for k in range(parts)
    ]
    inputs = [where, *returned, *([gate] * parts), *([joined] * parts)]
    aliases = {}
    if earlier is not None:
        aliases = {len(inputs): 0}
        inputs.append(earlier)
        specs.append(pl.BlockSpec(memory_space=pl.ANY))
    return pl.pallas_call(
        functools.partial(norm_body, parts, group, local_groups),
        grid_spec=pltpu.PrefetchScalarGridSpec(
            num_scalar_prefetch=1,
            grid=(steps,),
            in_specs=specs,
            out_specs=pl.BlockSpec(memory_space=pl.ANY),
            scratch_shapes=[
                pltpu.VMEM((steps, parts, step, width), jnp.bfloat16),
                pltpu.SemaphoreType.DMA((steps, parts)),
            ],
        ),
        out_shape=jax.ShapeDtypeStruct(gate.shape, jnp.bfloat16),
        input_output_aliases=aliases,
        compiler_params=params(),
        cost_estimate=cost(3),
    )(*inputs)


def place_body(where_ref, in_ref, out_ref):
    parts, rows, width = in_ref.shape
    alive = lax.broadcasted_iota(jnp.int32, (rows, 1), 0) + pl.program_id(0) * rows < where_ref[1]
    for part in range(parts):
        value = in_ref[part].astype(jnp.float32)
        out_ref[:, part * width : (part + 1) * width] = jnp.where(alive, value, 0.0).astype(jnp.bfloat16)


def place_heads(returned, where):
    parts, rows, width = returned.shape
    step = rows // 2
    return pl.pallas_call(
        place_body,
        grid_spec=pltpu.PrefetchScalarGridSpec(
            num_scalar_prefetch=1,
            grid=(rows // step,),
            in_specs=[pl.BlockSpec((parts, step, width), lambda i, *_: (0, i, 0))],
            out_specs=pl.BlockSpec((step, parts * width), lambda i, *_: (i, 0)),
        ),
        out_shape=jax.ShapeDtypeStruct((rows, parts * width), jnp.bfloat16),
        compiler_params=params(),
        cost_estimate=cost(2),
    )(where, returned)


def per_device(
    ssm_input,
    ssm_gate,
    state_proj,
    step_raw,
    queries,
    fresh_kv,
    block_pool,
    state_pool,
    decay_log,
    step_bias,
    skip_gain,
    norm_gain,
    block_owner,
    block_slot,
    block_count,
    state_entry,
    suffix_len,
):
    request = lax.axis_index("req")
    share = lax.axis_index("tp")
    parts = lax.axis_size("tp")
    owners = lax.axis_size("req")
    rows = ssm_input.shape[1]
    groups = state_proj.shape[2] // (2 * STATE)
    local_groups = groups // parts
    group_width = ssm_input.shape[2] // groups
    head_total = step_raw.shape[2]
    heads = head_total // groups
    channels = group_width // heads
    q_width = queries.shape[2] // parts
    fresh_width = fresh_kv.shape[2] // parts
    pool_local = block_pool.shape[0]
    pool_total = pool_local * owners
    listed = min(block_owner.shape[1], pool_total)
    order = bit_order(owners, 0)
    first_bit = 1 << order[0]

    pieces = [
        (ssm_input[0], local_groups * group_width, lambda p: p),
        (state_proj[0], local_groups * 2 * STATE, lambda p: p),
        (queries[0], q_width, lambda p: p),
        (fresh_kv[0], fresh_width, lambda p: p),
        (step_raw[0], head_total, lambda p: 0),
    ]
    q_column = pieces[0][1] + pieces[1][1]
    step_column = q_column + q_width + fresh_width
    pool_own = jnp.transpose(block_pool, (0, 2, 1, 3))
    state_own = state_pool.reshape(local_groups * group_width, STATE)
    state_groups = [state_own[group * group_width : (group + 1) * group_width] for group in range(local_groups)]
    packed = pack(parts, pieces, after(norm_gain, pool_own, *state_groups).reshape(-1, 128))
    joined = spread(packed)

    far_mask = 1 << order[1]
    state_far = swap(state_own, "req", far_mask)
    pool_far = after(swap(pool_own, "req", first_bit), packed)
    pool_held = join(pool_own, pool_far)
    pools = [(pool_held, [0, first_bit])]
    for bit in [order[-1]] + order[1:-1]:
        mask = 1 << bit
        moved = []
        for index, (array, held) in enumerate(pools):
            gate = [state_far] if mask == far_mask and index > 0 else []
            moved.append((swap(after(array, *gate), "req", mask), [offset ^ mask for offset in held]))
        pools += moved

    entries = after(state_entry, pool_held)
    state_lists, begun, late_gate = [None] * local_groups, [], [array for array, _ in pools[1:3]]
    for group in reversed(range(local_groups)):
        gates = ([pool_far], late_gate) if group % 2 == 0 else ([], [])
        source, values, sent = fetch_state(
            state_groups[group], state_far, far_mask, entries, bit_order(owners, group), *gates, group
        )
        state_lists[group] = (source, values)
        begun.append(sent)
        late_gate = late_gate + [values[-2]]

    targets = after(block_owner, pool_held)[request] * pool_local + block_slot[request]
    often, place, total = block_places(targets, block_count[request], pool_total)
    where = jnp.stack([request, total]).astype(jnp.int32)
    live = jnp.stack([share, suffix_len[request] - share * rows]).astype(jnp.int32)

    where = after(where, *begun[:-1])
    mixed = attention(joined, pools, where, often, place, listed, q_column, q_width)
    attn_back = spread(mixed)

    ssm_out = None
    skips = jnp.repeat(skip_gain, channels)[None, :]
    for group in reversed(range(local_groups)):
        mine = slice(group * heads, (group + 1) * heads)
        head_rows = jnp.zeros((8, head_total), jnp.float32)
        head_rows = head_rows.at[0, :heads].set(decay_log[mine])
        head_rows = head_rows.at[1, :heads].set(step_bias[mine])
        start = (share * local_groups + group) * heads
        shift = lax.rem(head_total - start, head_total)
        cols = slice(group * group_width, (group + 1) * group_width)
        source, values = state_lists[group]
        where = after(jnp.stack([share, shift, source]).astype(jnp.int32), mixed)
        scanned = scan_group(
            joined, step_column, values, where, head_rows, skips[:, cols], heads, group, local_groups
        )
        if group == 0:
            attn_out = place_heads(attn_back, after(live, scanned[0]))
            live = after(live, attn_out)
        ssm_out = norm_group(exchange(scanned), ssm_gate[0], joined, live, group, local_groups, ssm_out)
    return (ssm_out[None], attn_out[None])


def solution(mesh):
    return jax.shard_map(
        per_device,
        mesh=mesh,
        in_specs=(
            P("req", "tp", None),
            P("req", "tp", None),
            P("req", "tp", None),
            P("req", "tp", None),
            P("req", "tp", None),
            P("req", "tp", None),
            P("req", None, "tp", None),
            P("req", "tp", None, None),
            P("tp"),
            P("tp"),
            P("tp"),
            P("tp"),
            P(),
            P(),
            P(),
            P(),
            P(),
        ),
        out_specs=(P("req", "tp", None), P("req", "tp", None)),
        check_vma=False,
    )
```

```python
import functools
import math

import jax
import jax.numpy as jnp
from jax import lax
from jax.experimental import pallas as pl
from jax.experimental.pallas import tpu as pltpu
from jax.sharding import PartitionSpec as P

STATE = 256
SPAN = 256
TILE = 256
VMEM = 60 * 1024 * 1024
SMALL = 8 * 1024 * 1024


def cost(microseconds=0.0):
    return pl.CostEstimate(
        flops=1024 + int(microseconds * 1.15e9), bytes_accessed=1024, transcendentals=0
    )


def params(limit=VMEM):
    return pltpu.CompilerParams(vmem_limit_bytes=limit)


def dot_nt(left, right):
    return lax.dot_general(left, right, (((1,), (1,)), ((), ())), preferred_element_type=jnp.float32)


def dot_tn(left, right):
    return lax.dot_general(left, right, (((0,), (0,)), ((), ())), preferred_element_type=jnp.float32)


def pack(parts, pieces, gain):
    rows = pieces[0][0].shape[0]
    widths = [width for _, width, _ in pieces]
    gain_rows, lanes = gain.shape
    total = sum(widths) + lanes

    def body(*refs):
        *piece_refs, gain_ref, out_ref = refs
        at = 0
        for ref, width in zip(piece_refs, widths):
            out_ref[:, at : at + width] = ref[...]
            at += width
        terms, rest = [], gain_ref[...]
        for _ in range(3):
            terms.append(rest.astype(jnp.bfloat16).astype(jnp.float32))
            rest = rest - terms[-1]
        terms.append(jnp.zeros((rows - 3 * gain_rows, lanes), jnp.float32))
        out_ref[:, at:] = jnp.concatenate(terms, axis=0).astype(jnp.bfloat16)

    specs = [
        pl.BlockSpec((rows, width), functools.partial(lambda place, p: (0, place(p)), place))
        for _, width, place in pieces
    ]
    return pl.pallas_call(
        body,
        grid=(parts,),
        in_specs=specs + [pl.BlockSpec(gain.shape, lambda p: (0, 0))],
        out_specs=pl.BlockSpec((None, rows, total), lambda p: (p, 0, 0)),
        out_shape=jax.ShapeDtypeStruct((parts, rows, total), jnp.bfloat16),
        compiler_params=params(),
        cost_estimate=cost(),
    )(*[array for array, _, _ in pieces], gain)


def spread(packed):
    return lax.all_to_all(packed, "tp", split_axis=0, concat_axis=0, tiled=True)


def swap(value, axis, mask):
    count = lax.axis_size(axis)
    return lax.ppermute(value, axis, [(i, i ^ mask) for i in range(count)])


def exchange(buffers):
    return [buffers[0]] + [swap(buffers[k], "tp", k) for k in range(1, len(buffers))]


def after(value, *others):
    return lax.optimization_barrier((value, *others))[0]


def join_body(one_ref, two_ref, out_ref):
    half = one_ref.shape[0]
    out_ref[:half] = one_ref[...]
    out_ref[half:] = two_ref[...]


def join(one, two):
    shape = (one.shape[0] + two.shape[0],) + one.shape[1:]
    return pl.pallas_call(
        join_body,
        out_shape=jax.ShapeDtypeStruct(shape, one.dtype),
        compiler_params=params(SMALL),
        cost_estimate=cost(15),
    )(one, two)


def block_places(targets, used_entries, pool_total):
    blocks = jnp.arange(pool_total, dtype=jnp.int32)
    live = jnp.arange(targets.shape[0]) < used_entries
    named = (targets[:, None] == blocks[None, :]) & live[:, None]
    often = jnp.sum(named.astype(jnp.int32), axis=0)
    used = often > 0
    place = jnp.sum((used[None, :] & (blocks[None, :] < blocks[:, None])).astype(jnp.int32), axis=1)
    total = jnp.sum(used.astype(jnp.int32))
    return often, place.astype(jnp.int32), total.astype(jnp.int32)


def attention_body(parts, pool_offsets, listed, size, where_ref, often_ref, place_ref, q_ref, fresh_ref, *refs):
    pool_refs = refs[: len(pool_offsets)]
    out_ref, key_ref, value_ref = refs[len(pool_offsets) :]
    rows = q_ref.shape[1]
    repeat = q_ref.shape[2] // size
    fresh, block = fresh_ref.shape[0], pool_refs[0].shape[1]
    prefix = listed * block
    scale = math.log2(math.e) / math.sqrt(size)
    request, total = where_ref[0], where_ref[1]

    for pool_ref, offsets in zip(pool_refs, pool_offsets):
        slots = pool_ref.shape[0] // len(offsets)
        for index, offset in enumerate(offsets):
            for slot in range(slots):
                number = (request ^ offset) * slots + slot
                times = often_ref[number]

                @pl.when(times > 0)
                def _(pool_ref=pool_ref, held=index * slots + slot, number=number, times=times):
                    at = pl.ds(pl.multiple_of(place_ref[number] * block, block), block)
                    pair = pool_ref[held]
                    often = times.astype(jnp.float32)
                    key_ref[at, :] = pair[:, :size]
                    value_ref[at, :size] = (pair[:, size:].astype(jnp.float32) * often).astype(jnp.bfloat16)
                    value_ref[at, size:] = jnp.full((block, size), often, jnp.float32).astype(jnp.bfloat16)

    def fill(step, carry):
        at = pl.ds(pl.multiple_of(step * block, block), block)
        key_ref[at, :] = key_ref[:block, :]
        value_ref[at, :] = jnp.zeros((block, 2 * size), jnp.bfloat16)
        return carry

    lax.fori_loop(total, listed, fill, 0)
    key_ref[prefix:, :] = fresh_ref[:, :size]
    value_ref[prefix:, :size] = fresh_ref[:, size:]
    value_ref[prefix:, size:] = jnp.ones((fresh, size), jnp.bfloat16)

    query_at = lax.broadcasted_iota(jnp.int32, (repeat, rows, rows), 1).reshape(repeat * rows, rows)
    below = lax.broadcasted_iota(jnp.int32, (repeat * rows, rows), 1) <= query_at

    def scores(k):
        queries = jnp.concatenate(
            [q_ref[k, :, head * size : (head + 1) * size] for head in range(repeat)], axis=0
        )
        whole = prefix + k * rows
        return dot_nt(queries, key_ref[:whole, :]), dot_nt(queries, key_ref[whole : whole + rows, :])

    following = scores(0)
    for k in range(parts):
        seen, edge = following
        if k + 1 < parts:
            following = scores(k + 1)
        whole = prefix + k * rows
        edge = jnp.where(below, edge, -jnp.inf)
        top = jnp.maximum(
            jnp.max(seen, axis=1, keepdims=True), jnp.max(edge, axis=1, keepdims=True)
        )
        seen = jnp.exp2((seen - top) * scale).astype(jnp.bfloat16)
        edge = jnp.exp2((edge - top) * scale).astype(jnp.bfloat16)
        mixed = jnp.dot(seen, value_ref[:whole, :], preferred_element_type=jnp.float32)
        mixed += jnp.dot(edge, value_ref[whole : whole + rows, :], preferred_element_type=jnp.float32)
        result = (mixed[:, :size] / mixed[:, size:]).astype(jnp.bfloat16)
        for head in range(repeat):
            out_ref[k, :, head * size : (head + 1) * size] = result[head * rows : (head + 1) * rows]


def attention(first, pools, where, often, place, listed, q_column, q_width):
    parts, rows, _ = first.shape
    _, kv_local, block, pair = pools[0][0].shape
    size = pair // 2
    per_kv = q_width // kv_local
    keys = listed * block + rows * parts
    specs = [
        pl.BlockSpec((parts, rows, per_kv), lambda c, *_: (0, 0, q_column // per_kv + c)),
        pl.BlockSpec((rows * parts, pair), lambda c, *_: (0, (q_column + q_width) // pair + c)),
    ]
    specs += [
        pl.BlockSpec((array.shape[0], None, block, pair), lambda c, *_: (0, c, 0, 0)) for array, _ in pools
    ]
    return pl.pallas_call(
        functools.partial(attention_body, parts, [offsets for _, offsets in pools], listed, size),
        grid_spec=pltpu.PrefetchScalarGridSpec(
            num_scalar_prefetch=3,
            grid=(kv_local,),
            in_specs=specs,
            out_specs=pl.BlockSpec((parts, rows, per_kv), lambda c, *_: (0, 0, c)),
            scratch_shapes=[
                pltpu.VMEM((keys, size), jnp.bfloat16),
                pltpu.VMEM((keys, 2 * size), jnp.bfloat16),
            ],
        ),
        out_shape=jax.ShapeDtypeStruct((parts, rows, q_width), jnp.bfloat16),
        compiler_params=params(),
        cost_estimate=cost(16),
    )(
        where,
        often,
        place,
        first,
        first.reshape(parts * rows, first.shape[2]),
        *[array for array, _ in pools],
    )


def scan_body(parts, sources, heads, group, where_ref, x_ref, proj_ref, raw_ref, head_ref, skip_ref, *refs):
    state_refs = refs[:sources]
    out_refs = refs[sources:-4]
    y_ref, state_ref, next_ref, sem = refs[-4:]
    share = where_ref[0]
    shift = where_ref[1]
    source = where_ref[2]
    rows, width = x_ref.shape
    for index in range(sources):

        @pl.when(source == index)
        def _(index=index):
            pltpu.make_async_copy(rows_of(state_refs[index], group, width), state_ref, sem).start()

    channels = width // heads
    lane = lax.broadcasted_iota(jnp.int32, (1, 2 * channels), 1)
    first_lanes = lane < channels
    row_at = lax.broadcasted_iota(jnp.int32, (2 * channels, 1), 0)
    first_rows = row_at < channels
    lower = lax.broadcasted_iota(jnp.int32, (SPAN, SPAN), 1) <= lax.broadcasted_iota(
        jnp.int32, (SPAN, SPAN), 0
    )
    base = math.log2(math.e)
    ones = jnp.where(lower, 1.0, 0.0)
    raw = pltpu.roll(raw_ref[...].astype(jnp.float32), shift, 1) + head_ref[1:2, :]
    step = jnp.maximum(raw, 0.0) + jnp.log1p(jnp.exp(-jnp.abs(raw)))
    rates = jnp.exp(head_ref[0:1, :])
    for start in range(0, rows, SPAN):
        at = slice(start, start + SPAN)
        last_block = start + SPAN >= rows
        step_block = step[at, :]
        cumul = jnp.dot(
            ones,
            -rates * step_block,
            precision=lax.Precision.HIGHEST,
            preferred_element_type=jnp.float32,
        )
        ahead = base * cumul
        back = jnp.transpose(base * (jnp.log(step_block) - cumul))
        grown = jnp.exp(cumul)
        final = cumul[SPAN - 1 : SPAN, :]
        tail = jnp.exp(final - cumul) * step_block
        kept = jnp.exp(final)
        b_block = proj_ref[at, :STATE]
        c_block = proj_ref[at, STATE:]
        inner = dot_nt(c_block, b_block)
        if start == 0:
            pltpu.make_async_copy(rows_of(state_refs[0], group, width), state_ref, sem).wait()
        state = state_ref if start == 0 else next_ref
        carried = dot_nt(c_block, state[...])
        for pair in range(heads // 2):
            cols = slice(pair * 2 * channels, (pair + 1) * 2 * channels)
            one, two = 2 * pair, 2 * pair + 1
            x_pair = x_ref[at, cols]
            mixings = []
            for head in (one, two):
                spread_at = ahead[:, head : head + 1] + back[head : head + 1, :]
                decay = jnp.exp2(jnp.where(lower, spread_at, -jnp.inf))
                mixings.append((decay * inner).astype(jnp.bfloat16))
            nothing = jnp.zeros_like(x_pair)
            output = jnp.dot(
                mixings[0], jnp.where(first_lanes, x_pair, nothing), preferred_element_type=jnp.float32
            )
            output += jnp.dot(
                mixings[1], jnp.where(first_lanes, nothing, x_pair), preferred_element_type=jnp.float32
            )
            x_wide = x_pair.astype(jnp.float32)
            factor = jnp.where(first_lanes, grown[:, one : one + 1], grown[:, two : two + 1])
            output += factor * carried[:, cols] + skip_ref[:, cols] * x_wide
            y_ref[at, cols] = output.astype(jnp.bfloat16)
            if not last_block:
                weight = jnp.where(first_lanes, tail[:, one : one + 1], tail[:, two : two + 1])
                terms = (weight * x_wide).astype(jnp.bfloat16)
                keep = jnp.where(first_rows, kept[:, one : one + 1], kept[:, two : two + 1])
                moved = keep * state[cols, :].astype(jnp.float32) + dot_tn(terms, b_block)
                next_ref[cols, :] = moved.astype(jnp.bfloat16)
    part_rows = rows // parts
    for k in range(parts):
        at = pl.ds(pl.multiple_of((share ^ k) * part_rows, part_rows), part_rows)
        out_refs[k][...] = y_ref[at, :]


def scan_group(joined, step_column, states, where, head_rows, skip_row, heads, group, local_groups):
    parts, part_rows, _ = joined.shape
    sources = len(states)
    rows = part_rows * parts
    width = skip_row.shape[1]
    step_width = head_rows.shape[1]
    proj_width = 2 * STATE
    specs = [
        pl.BlockSpec((rows, width), lambda i, *_: (0, group)),
        pl.BlockSpec((rows, proj_width), lambda i, *_: (0, local_groups * width // proj_width + group)),
        pl.BlockSpec((rows, step_width), lambda i, *_: (0, step_column // step_width)),
        pl.BlockSpec((8, step_width), lambda i, *_: (0, 0)),
        pl.BlockSpec((1, width), lambda i, *_: (0, 0)),
    ]
    specs += [pl.BlockSpec(memory_space=pl.ANY)] * sources
    flat = joined.reshape(rows, joined.shape[2])
    return pl.pallas_call(
        functools.partial(scan_body, parts, sources, heads, group),
        grid_spec=pltpu.PrefetchScalarGridSpec(
            num_scalar_prefetch=1,
            grid=(1,),
            in_specs=specs,
            out_specs=[pl.BlockSpec((part_rows, width), lambda i, *_: (0, 0))] * parts,
            scratch_shapes=[
                pltpu.VMEM((rows, width), jnp.bfloat16),
                pltpu.VMEM((width, STATE), jnp.bfloat16),
                pltpu.VMEM((width, STATE), jnp.bfloat16),
                pltpu.SemaphoreType.DMA,
            ],
        ),
        out_shape=[jax.ShapeDtypeStruct((part_rows, width), jnp.bfloat16)] * parts,
        compiler_params=params(),
        cost_estimate=cost(8),
    )(where, flat, flat, flat, head_rows, skip_row, *states)


def rows_of(ref, group, size):
    return ref if ref.shape[0] == size else ref.at[group * size : (group + 1) * size]


def choose_body(sources, group, index_ref, *refs):
    out_ref, sem = refs[sources:]
    size = out_ref.shape[0]
    for index in range(sources):

        @pl.when(index_ref[0] == index)
        def _(index=index):
            pltpu.make_async_copy(rows_of(refs[index], group, size), out_ref, sem).start()

    pltpu.make_async_copy(rows_of(refs[0], group, size), out_ref, sem).wait()


def choose(index, arrays, group, size):
    return pl.pallas_call(
        functools.partial(choose_body, len(arrays), group),
        grid_spec=pltpu.PrefetchScalarGridSpec(
            num_scalar_prefetch=1,
            grid=(1,),
            in_specs=[pl.BlockSpec(memory_space=pl.ANY)] * len(arrays),
            out_specs=pl.BlockSpec((size, STATE), lambda i, *_: (0, 0)),
            scratch_shapes=[pltpu.SemaphoreType.DMA],
        ),
        out_shape=jax.ShapeDtypeStruct((size, STATE), jnp.bfloat16),
        compiler_params=params(SMALL),
        cost_estimate=cost(),
    )(index, *arrays)


def bit_order(count, group):
    bits = count.bit_length() - 1
    if group % 2 == 0:
        return [bits - 1] + list(range(bits - 1))
    return [bits - 2] + list(range(bits - 2)) + [bits - 1]


def slot_of(distance, offsets):
    return sum(jnp.where(distance == offset, i, 0) for i, offset in enumerate(offsets))


def fetch_state(own, far, far_mask, entries, order, gate, late_gate, last_gate, group):
    count = lax.axis_size("req")
    size = own.shape[0]
    offsets, held = [0], [own]
    for step, bit in enumerate(order[:-1]):
        mask = 1 << bit
        moved = []
        for offset, value in zip(offsets, held):
            if offset == 0 and mask == far_mask:
                moved.append(far)
            else:
                moved.append(swap(after(value, *(late_gate if step else gate)), "req", mask))
        held = held + moved
        offsets = offsets + [offset ^ mask for offset in offsets]
    last = 1 << order[-1]
    every = jnp.arange(count, dtype=jnp.int32)
    bits = len(order)
    flipped = jnp.flip(entries.reshape((2,) * bits), bits - 1 - order[-1]).reshape(count)
    distance = entries ^ every
    source = jnp.where((distance & last) == 0, slot_of(distance, offsets), len(held))
    choices = jnp.stack([slot_of(flipped ^ every, offsets), source]).astype(jnp.int32)
    mine = lax.dynamic_slice_in_dim(choices, lax.axis_index("req"), 1, axis=1)[:, 0]
    begun = choose(after(mine[0:1], *last_gate), held, group, size)
    return mine[1], held + [swap(begun, "req", last)], begun


def norm_body(parts, group, local_groups, where_ref, *refs):
    y_refs = refs[:parts]
    gate_refs = refs[parts : 2 * parts]
    gain_refs = refs[2 * parts : 3 * parts]
    out_ref, done_ref, sem = refs[-3:]
    share, live = where_ref[0], where_ref[1]
    number, steps = pl.program_id(0), pl.num_programs(0)
    rows, width = y_refs[0].shape
    row_at = lax.broadcasted_iota(jnp.int32, (rows, 1), 0) + number * rows
    lanes = gain_refs[0].shape[1]
    chunks = width // lanes
    third = chunks * local_groups

    def placing(step, k):
        column = pl.multiple_of(((share ^ k) * local_groups + group) * width, width)
        at = pl.ds(pl.multiple_of(step * rows, rows), rows)
        return pltpu.make_async_copy(done_ref.at[step, k], out_ref.at[at, pl.ds(column, width)], sem.at[step, k])

    for k in range(parts):
        gate = gate_refs[k][...].astype(jnp.float32)
        gated = y_refs[k][...].astype(jnp.float32) * gate * (0.5 + 0.5 * jnp.tanh(0.5 * gate))
        mean_sq = jnp.mean(gated * gated, axis=1, keepdims=True)
        normed = gated * jnp.where(row_at < live, lax.rsqrt(mean_sq + 1e-05), 0.0)
        gains = gain_refs[k][...].astype(jnp.float32)
        first = group * chunks
        gain = sum(gains[first + i * third : first + i * third + chunks] for i in range(3))
        for chunk in range(chunks):
            cols = slice(chunk * lanes, (chunk + 1) * lanes)
            done_ref[number, k, :, cols] = (normed[:, cols] * gain[chunk : chunk + 1, :]).astype(jnp.bfloat16)
        placing(number, k).start()

    @pl.when(number == steps - 1)
    def _():
        for step in range(done_ref.shape[0]):
            for k in range(parts):
                placing(step, k).wait()


def norm_group(returned, gate, joined, where, group, local_groups, earlier):
    parts = joined.shape[0]
    rows, width = returned[0].shape[-2:]
    lanes, steps = 128, 2
    step = rows // steps
    specs = [pl.BlockSpec((step, width), lambda i, *_: (i, 0))] * parts
    specs += [
        pl.BlockSpec((step, width), functools.partial(lambda k, i, at: (i, (at[0] ^ k) * local_groups + group), k))
        for k in range(parts)
    ]
    specs += [
        pl.BlockSpec(
            (None, rows, lanes),
            functools.partial(lambda k, i, at: (at[0] ^ k, 0, joined.shape[2] // lanes - 1), k),
        )
        for k in range(parts)
    ]
    inputs = [where, *returned, *([gate] * parts), *([joined] * parts)]
    aliases = {}
    if earlier is not None:
        aliases = {len(inputs): 0}
        inputs.append(earlier)
        specs.append(pl.BlockSpec(memory_space=pl.ANY))
    return pl.pallas_call(
        functools.partial(norm_body, parts, group, local_groups),
        grid_spec=pltpu.PrefetchScalarGridSpec(
            num_scalar_prefetch=1,
            grid=(steps,),
            in_specs=specs,
            out_specs=pl.BlockSpec(memory_space=pl.ANY),
            scratch_shapes=[
                pltpu.VMEM((steps, parts, step, width), jnp.bfloat16),
                pltpu.SemaphoreType.DMA((steps, parts)),
            ],
        ),
        out_shape=jax.ShapeDtypeStruct(gate.shape, jnp.bfloat16),
        input_output_aliases=aliases,
        compiler_params=params(),
        cost_estimate=cost(3),
    )(*inputs)


def place_body(where_ref, in_ref, out_ref):
    parts, rows, width = in_ref.shape
    alive = lax.broadcasted_iota(jnp.int32, (rows, 1), 0) + pl.program_id(0) * rows < where_ref[1]
    for part in range(parts):
        value = in_ref[part].astype(jnp.float32)
        out_ref[:, part * width : (part + 1) * width] = jnp.where(alive, value, 0.0).astype(jnp.bfloat16)


def place_heads(returned, where):
    parts, rows, width = returned.shape
    step = rows // 2
    return pl.pallas_call(
        place_body,
        grid_spec=pltpu.PrefetchScalarGridSpec(
            num_scalar_prefetch=1,
            grid=(rows // step,),
            in_specs=[pl.BlockSpec((parts, step, width), lambda i, *_: (0, i, 0))],
            out_specs=pl.BlockSpec((step, parts * width), lambda i, *_: (i, 0)),
        ),
        out_shape=jax.ShapeDtypeStruct((rows, parts * width), jnp.bfloat16),
        compiler_params=params(),
        cost_estimate=cost(2),
    )(where, returned)


def per_device(
    ssm_input,
    ssm_gate,
    state_proj,
    step_raw,
    queries,
    fresh_kv,
    block_pool,
    state_pool,
    decay_log,
    step_bias,
    skip_gain,
    norm_gain,
    block_owner,
    block_slot,
    block_count,
    state_entry,
    suffix_len,
):
    request = lax.axis_index("req")
    share = lax.axis_index("tp")
    parts = lax.axis_size("tp")
    owners = lax.axis_size("req")
    rows = ssm_input.shape[1]
    groups = state_proj.shape[2] // (2 * STATE)
    local_groups = groups // parts
    group_width = ssm_input.shape[2] // groups
    head_total = step_raw.shape[2]
    heads = head_total // groups
    channels = group_width // heads
    q_width = queries.shape[2] // parts
    fresh_width = fresh_kv.shape[2] // parts
    pool_local = block_pool.shape[0]
    pool_total = pool_local * owners
    listed = min(block_owner.shape[1], pool_total)
    order = bit_order(owners, 0)
    first_bit = 1 << order[0]

    pieces = [
        (ssm_input[0], local_groups * group_width, lambda p: p),
        (state_proj[0], local_groups * 2 * STATE, lambda p: p),
        (queries[0], q_width, lambda p: p),
        (fresh_kv[0], fresh_width, lambda p: p),
        (step_raw[0], head_total, lambda p: 0),
    ]
    q_column = pieces[0][1] + pieces[1][1]
    step_column = q_column + q_width + fresh_width
    pool_own = jnp.transpose(block_pool, (0, 2, 1, 3))
    state_own = state_pool.reshape(local_groups * group_width, STATE)
    state_groups = [state_own[group * group_width : (group + 1) * group_width] for group in range(local_groups)]
    packed = pack(parts, pieces, after(norm_gain, pool_own, *state_groups).reshape(-1, 128))
    joined = spread(packed)

    far_mask = 1 << order[1]
    state_far = swap(state_own, "req", far_mask)
    pool_far = after(swap(pool_own, "req", first_bit), packed)
    pool_held = join(pool_own, pool_far)
    pools = [(pool_held, [0, first_bit])]
    for bit in [order[-1]] + order[1:-1]:
        mask = 1 << bit
        moved = []
        for index, (array, held) in enumerate(pools):
            gate = [state_far] if mask == far_mask and index > 0 else []
            moved.append((swap(after(array, *gate), "req", mask), [offset ^ mask for offset in held]))
        pools += moved

    entries = after(state_entry, pool_held)
    state_lists, begun = [None] * local_groups, []

    def fetch(group, last_gate):
        gates = ([pools[1][0]], [pools[2][0]]) if group % 2 == 0 else ([], [])
        source, values, sent = fetch_state(
            state_groups[group], state_far, far_mask, entries, bit_order(owners, group), *gates, last_gate, group
        )
        state_lists[group] = (source, values)
        begun.append(sent)

    for group in reversed(range(1, local_groups)):
        fetch(group, [])

    targets = after(block_owner, pool_held)[request] * pool_local + block_slot[request]
    often, place, total = block_places(targets, block_count[request], pool_total)
    where = jnp.stack([request, total]).astype(jnp.int32)
    live = jnp.stack([share, suffix_len[request] - share * rows]).astype(jnp.int32)

    where = after(where, *begun)
    mixed = attention(joined, pools, where, often, place, listed, q_column, q_width)
    attn_back = spread(mixed)
    fetch(0, [mixed])

    ssm_out = None
    skips = jnp.repeat(skip_gain, channels)[None, :]
    for group in reversed(range(local_groups)):
        mine = slice(group * heads, (group + 1) * heads)
        head_rows = jnp.zeros((8, head_total), jnp.float32)
        head_rows = head_rows.at[0, :heads].set(decay_log[mine])
        head_rows = head_rows.at[1, :heads].set(step_bias[mine])
        start = (share * local_groups + group) * heads
        shift = lax.rem(head_total - start, head_total)
        cols = slice(group * group_width, (group + 1) * group_width)
        source, values = state_lists[group]
        where = after(jnp.stack([share, shift, source]).astype(jnp.int32), mixed, begun[-1])
        scanned = scan_group(
            joined, step_column, values, where, head_rows, skips[:, cols], heads, group, local_groups
        )
        if group == 0:
            attn_out = place_heads(attn_back, after(live, scanned[0]))
            live = after(live, attn_out)
        ssm_out = norm_group(exchange(scanned), ssm_gate[0], joined, live, group, local_groups, ssm_out)
    return (ssm_out[None], attn_out[None])


def solution(mesh):
    return jax.shard_map(
        per_device,
        mesh=mesh,
        in_specs=(
            P("req", "tp", None),
            P("req", "tp", None),
            P("req", "tp", None),
            P("req", "tp", None),
            P("req", "tp", None),
            P("req", "tp", None),
            P("req", None, "tp", None),
            P("req", "tp", None, None),
            P("tp"),
            P("tp"),
            P("tp"),
            P("tp"),
            P(),
            P(),
            P(),
            P(),
            P(),
        ),
        out_specs=(P("req", "tp", None), P("req", "tp", None)),
        check_vma=False,
    )
```

```python
import functools
import math

import jax
import jax.numpy as jnp
from jax import lax
from jax.experimental import pallas as pl
from jax.experimental.pallas import tpu as pltpu
from jax.sharding import PartitionSpec as P

STATE = 256
SPAN = 256
TILE = 256
VMEM = 60 * 1024 * 1024
SMALL = 8 * 1024 * 1024


def cost(microseconds=0.0):
    return pl.CostEstimate(
        flops=1024 + int(microseconds * 1.15e9), bytes_accessed=1024, transcendentals=0
    )


def params(limit=VMEM):
    return pltpu.CompilerParams(vmem_limit_bytes=limit)


def dot_nt(left, right):
    return lax.dot_general(left, right, (((1,), (1,)), ((), ())), preferred_element_type=jnp.float32)


def dot_tn(left, right):
    return lax.dot_general(left, right, (((0,), (0,)), ((), ())), preferred_element_type=jnp.float32)


def pack(parts, pieces, gain):
    rows = pieces[0][0].shape[0]
    widths = [width for _, width, _ in pieces]
    gain_rows, lanes = gain.shape
    total = sum(widths) + lanes

    def body(*refs):
        *piece_refs, gain_ref, out_ref = refs
        at = 0
        for ref, width in zip(piece_refs, widths):
            out_ref[:, at : at + width] = ref[...]
            at += width
        terms, rest = [], gain_ref[...]
        for _ in range(3):
            terms.append(rest.astype(jnp.bfloat16).astype(jnp.float32))
            rest = rest - terms[-1]
        terms.append(jnp.zeros((rows - 3 * gain_rows, lanes), jnp.float32))
        out_ref[:, at:] = jnp.concatenate(terms, axis=0).astype(jnp.bfloat16)

    specs = [
        pl.BlockSpec((rows, width), functools.partial(lambda place, p: (0, place(p)), place))
        for _, width, place in pieces
    ]
    return pl.pallas_call(
        body,
        grid=(parts,),
        in_specs=specs + [pl.BlockSpec(gain.shape, lambda p: (0, 0))],
        out_specs=pl.BlockSpec((None, rows, total), lambda p: (p, 0, 0)),
        out_shape=jax.ShapeDtypeStruct((parts, rows, total), jnp.bfloat16),
        compiler_params=params(),
        cost_estimate=cost(),
    )(*[array for array, _, _ in pieces], gain)


def spread(packed):
    return lax.all_to_all(packed, "tp", split_axis=0, concat_axis=0, tiled=True)


def swap(value, axis, mask):
    count = lax.axis_size(axis)
    return lax.ppermute(value, axis, [(i, i ^ mask) for i in range(count)])


def exchange(buffers):
    return [buffers[0]] + [swap(buffers[k], "tp", k) for k in range(1, len(buffers))]


def after(value, *others):
    return lax.optimization_barrier((value, *others))[0]


def join_body(one_ref, two_ref, out_ref):
    half = one_ref.shape[0]
    out_ref[:half] = one_ref[...]
    out_ref[half:] = two_ref[...]


def join(one, two):
    shape = (one.shape[0] + two.shape[0],) + one.shape[1:]
    return pl.pallas_call(
        join_body,
        out_shape=jax.ShapeDtypeStruct(shape, one.dtype),
        compiler_params=params(SMALL),
        cost_estimate=cost(15),
    )(one, two)


def block_places(targets, used_entries, pool_total):
    blocks = jnp.arange(pool_total, dtype=jnp.int32)
    live = jnp.arange(targets.shape[0]) < used_entries
    named = (targets[:, None] == blocks[None, :]) & live[:, None]
    often = jnp.sum(named.astype(jnp.int32), axis=0)
    used = often > 0
    place = jnp.sum((used[None, :] & (blocks[None, :] < blocks[:, None])).astype(jnp.int32), axis=1)
    total = jnp.sum(used.astype(jnp.int32))
    return often, place.astype(jnp.int32), total.astype(jnp.int32)


def attention_body(parts, pool_offsets, listed, size, where_ref, often_ref, place_ref, q_ref, fresh_ref, *refs):
    pool_refs = refs[: len(pool_offsets)]
    out_ref, key_ref, value_ref = refs[len(pool_offsets) :]
    rows = q_ref.shape[1]
    repeat = q_ref.shape[2] // size
    fresh, block = fresh_ref.shape[0], pool_refs[0].shape[1]
    prefix = listed * block
    scale = math.log2(math.e) / math.sqrt(size)
    request, total = where_ref[0], where_ref[1]

    for pool_ref, offsets in zip(pool_refs, pool_offsets):
        slots = pool_ref.shape[0] // len(offsets)
        for index, offset in enumerate(offsets):
            for slot in range(slots):
                number = (request ^ offset) * slots + slot
                times = often_ref[number]

                @pl.when(times > 0)
                def _(pool_ref=pool_ref, held=index * slots + slot, number=number, times=times):
                    at = pl.ds(pl.multiple_of(place_ref[number] * block, block), block)
                    pair = pool_ref[held]
                    often = times.astype(jnp.float32)
                    key_ref[at, :] = pair[:, :size]
                    value_ref[at, :size] = (pair[:, size:].astype(jnp.float32) * often).astype(jnp.bfloat16)
                    value_ref[at, size:] = jnp.full((block, size), often, jnp.float32).astype(jnp.bfloat16)

    def fill(step, carry):
        at = pl.ds(pl.multiple_of(step * block, block), block)
        key_ref[at, :] = key_ref[:block, :]
        value_ref[at, :] = jnp.zeros((block, 2 * size), jnp.bfloat16)
        return carry

    lax.fori_loop(total, listed, fill, 0)
    key_ref[prefix:, :] = fresh_ref[:, :size]
    value_ref[prefix:, :size] = fresh_ref[:, size:]
    value_ref[prefix:, size:] = jnp.ones((fresh, size), jnp.bfloat16)

    query_at = lax.broadcasted_iota(jnp.int32, (repeat, rows, rows), 1).reshape(repeat * rows, rows)
    below = lax.broadcasted_iota(jnp.int32, (repeat * rows, rows), 1) <= query_at

    def scores(k):
        queries = jnp.concatenate(
            [q_ref[k, :, head * size : (head + 1) * size] for head in range(repeat)], axis=0
        )
        whole = prefix + k * rows
        return dot_nt(queries, key_ref[:whole, :]), dot_nt(queries, key_ref[whole : whole + rows, :])

    following = scores(0)
    for k in range(parts):
        seen, edge = following
        if k + 1 < parts:
            following = scores(k + 1)
        whole = prefix + k * rows
        edge = jnp.where(below, edge, -jnp.inf)
        top = jnp.maximum(
            jnp.max(seen, axis=1, keepdims=True), jnp.max(edge, axis=1, keepdims=True)
        )
        seen = jnp.exp2((seen - top) * scale).astype(jnp.bfloat16)
        edge = jnp.exp2((edge - top) * scale).astype(jnp.bfloat16)
        mixed = jnp.dot(seen, value_ref[:whole, :], preferred_element_type=jnp.float32)
        mixed += jnp.dot(edge, value_ref[whole : whole + rows, :], preferred_element_type=jnp.float32)
        result = (mixed[:, :size] / mixed[:, size:]).astype(jnp.bfloat16)
        for head in range(repeat):
            out_ref[k, :, head * size : (head + 1) * size] = result[head * rows : (head + 1) * rows]


def attention(first, pools, where, often, place, listed, q_column, q_width):
    parts, rows, _ = first.shape
    _, kv_local, block, pair = pools[0][0].shape
    size = pair // 2
    per_kv = q_width // kv_local
    keys = listed * block + rows * parts
    specs = [
        pl.BlockSpec((parts, rows, per_kv), lambda c, *_: (0, 0, q_column // per_kv + c)),
        pl.BlockSpec((rows * parts, pair), lambda c, *_: (0, (q_column + q_width) // pair + c)),
    ]
    specs += [
        pl.BlockSpec((array.shape[0], None, block, pair), lambda c, *_: (0, c, 0, 0)) for array, _ in pools
    ]
    return pl.pallas_call(
        functools.partial(attention_body, parts, [offsets for _, offsets in pools], listed, size),
        grid_spec=pltpu.PrefetchScalarGridSpec(
            num_scalar_prefetch=3,
            grid=(kv_local,),
            in_specs=specs,
            out_specs=pl.BlockSpec((parts, rows, per_kv), lambda c, *_: (0, 0, c)),
            scratch_shapes=[
                pltpu.VMEM((keys, size), jnp.bfloat16),
                pltpu.VMEM((keys, 2 * size), jnp.bfloat16),
            ],
        ),
        out_shape=jax.ShapeDtypeStruct((parts, rows, q_width), jnp.bfloat16),
        compiler_params=params(),
        cost_estimate=cost(16),
    )(
        where,
        often,
        place,
        first,
        first.reshape(parts * rows, first.shape[2]),
        *[array for array, _ in pools],
    )


def scan_body(parts, sources, heads, group, where_ref, x_ref, proj_ref, raw_ref, head_ref, skip_ref, *refs):
    state_refs = refs[:sources]
    out_refs = refs[sources:-4]
    y_ref, state_ref, next_ref, sem = refs[-4:]
    share = where_ref[0]
    shift = where_ref[1]
    source = where_ref[2]
    rows, width = x_ref.shape
    for index in range(sources):

        @pl.when(source == index)
        def _(index=index):
            pltpu.make_async_copy(rows_of(state_refs[index], group, width), state_ref, sem).start()

    channels = width // heads
    lane = lax.broadcasted_iota(jnp.int32, (1, 2 * channels), 1)
    first_lanes = lane < channels
    row_at = lax.broadcasted_iota(jnp.int32, (2 * channels, 1), 0)
    first_rows = row_at < channels
    lower = lax.broadcasted_iota(jnp.int32, (SPAN, SPAN), 1) <= lax.broadcasted_iota(
        jnp.int32, (SPAN, SPAN), 0
    )
    base = math.log2(math.e)
    ones = jnp.where(lower, 1.0, 0.0)
    raw = pltpu.roll(raw_ref[...].astype(jnp.float32), shift, 1) + head_ref[1:2, :]
    step = jnp.maximum(raw, 0.0) + jnp.log1p(jnp.exp(-jnp.abs(raw)))
    rates = jnp.exp(head_ref[0:1, :])
    for start in range(0, rows, SPAN):
        at = slice(start, start + SPAN)
        last_block = start + SPAN >= rows
        step_block = step[at, :]
        cumul = jnp.dot(
            ones,
            -rates * step_block,
            precision=lax.Precision.HIGHEST,
            preferred_element_type=jnp.float32,
        )
        ahead = base * cumul
        back = jnp.transpose(base * (jnp.log(step_block) - cumul))
        grown = jnp.exp(cumul)
        final = cumul[SPAN - 1 : SPAN, :]
        tail = jnp.exp(final - cumul) * step_block
        kept = jnp.exp(final)
        b_block = proj_ref[at, :STATE]
        c_block = proj_ref[at, STATE:]
        inner = dot_nt(c_block, b_block)
        if start == 0:
            pltpu.make_async_copy(rows_of(state_refs[0], group, width), state_ref, sem).wait()
        state = state_ref if start == 0 else next_ref
        carried = dot_nt(c_block, state[...])
        for pair in range(heads // 2):
            cols = slice(pair * 2 * channels, (pair + 1) * 2 * channels)
            one, two = 2 * pair, 2 * pair + 1
            x_pair = x_ref[at, cols]
            mixings = []
            for head in (one, two):
                spread_at = ahead[:, head : head + 1] + back[head : head + 1, :]
                decay = jnp.exp2(jnp.where(lower, spread_at, -jnp.inf))
                mixings.append((decay * inner).astype(jnp.bfloat16))
            nothing = jnp.zeros_like(x_pair)
            output = jnp.dot(
                mixings[0], jnp.where(first_lanes, x_pair, nothing), preferred_element_type=jnp.float32
            )
            output += jnp.dot(
                mixings[1], jnp.where(first_lanes, nothing, x_pair), preferred_element_type=jnp.float32
            )
            x_wide = x_pair.astype(jnp.float32)
            factor = jnp.where(first_lanes, grown[:, one : one + 1], grown[:, two : two + 1])
            output += factor * carried[:, cols] + skip_ref[:, cols] * x_wide
            y_ref[at, cols] = output.astype(jnp.bfloat16)
            if not last_block:
                weight = jnp.where(first_lanes, tail[:, one : one + 1], tail[:, two : two + 1])
                terms = (weight * x_wide).astype(jnp.bfloat16)
                keep = jnp.where(first_rows, kept[:, one : one + 1], kept[:, two : two + 1])
                moved = keep * state[cols, :].astype(jnp.float32) + dot_tn(terms, b_block)
                next_ref[cols, :] = moved.astype(jnp.bfloat16)
    part_rows = rows // parts
    for k in range(parts):
        at = pl.ds(pl.multiple_of((share ^ k) * part_rows, part_rows), part_rows)
        out_refs[k][...] = y_ref[at, :]


def scan_group(joined, step_column, states, where, head_rows, skip_row, heads, group, local_groups):
    parts, part_rows, _ = joined.shape
    sources = len(states)
    rows = part_rows * parts
    width = skip_row.shape[1]
    step_width = head_rows.shape[1]
    proj_width = 2 * STATE
    specs = [
        pl.BlockSpec((rows, width), lambda i, *_: (0, group)),
        pl.BlockSpec((rows, proj_width), lambda i, *_: (0, local_groups * width // proj_width + group)),
        pl.BlockSpec((rows, step_width), lambda i, *_: (0, step_column // step_width)),
        pl.BlockSpec((8, step_width), lambda i, *_: (0, 0)),
        pl.BlockSpec((1, width), lambda i, *_: (0, 0)),
    ]
    specs += [pl.BlockSpec(memory_space=pl.ANY)] * sources
    flat = joined.reshape(rows, joined.shape[2])
    return pl.pallas_call(
        functools.partial(scan_body, parts, sources, heads, group),
        grid_spec=pltpu.PrefetchScalarGridSpec(
            num_scalar_prefetch=1,
            grid=(1,),
            in_specs=specs,
            out_specs=[pl.BlockSpec((part_rows, width), lambda i, *_: (0, 0))] * parts,
            scratch_shapes=[
                pltpu.VMEM((rows, width), jnp.bfloat16),
                pltpu.VMEM((width, STATE), jnp.bfloat16),
                pltpu.VMEM((width, STATE), jnp.bfloat16),
                pltpu.SemaphoreType.DMA,
            ],
        ),
        out_shape=[jax.ShapeDtypeStruct((part_rows, width), jnp.bfloat16)] * parts,
        compiler_params=params(),
        cost_estimate=cost(8),
    )(where, flat, flat, flat, head_rows, skip_row, *states)


def rows_of(ref, group, size):
    return ref if ref.shape[0] == size else ref.at[group * size : (group + 1) * size]


def choose_body(sources, group, index_ref, *refs):
    out_ref, sem = refs[sources:]
    size = out_ref.shape[0]
    for index in range(sources):

        @pl.when(index_ref[0] == index)
        def _(index=index):
            pltpu.make_async_copy(rows_of(refs[index], group, size), out_ref, sem).start()

    pltpu.make_async_copy(rows_of(refs[0], group, size), out_ref, sem).wait()


def choose(index, arrays, group, size):
    return pl.pallas_call(
        functools.partial(choose_body, len(arrays), group),
        grid_spec=pltpu.PrefetchScalarGridSpec(
            num_scalar_prefetch=1,
            grid=(1,),
            in_specs=[pl.BlockSpec(memory_space=pl.ANY)] * len(arrays),
            out_specs=pl.BlockSpec((size, STATE), lambda i, *_: (0, 0)),
            scratch_shapes=[pltpu.SemaphoreType.DMA],
        ),
        out_shape=jax.ShapeDtypeStruct((size, STATE), jnp.bfloat16),
        compiler_params=params(SMALL),
        cost_estimate=cost(),
    )(index, *arrays)


def bit_order(count, group):
    bits = count.bit_length() - 1
    if group % 2 == 0:
        return [bits - 1] + list(range(bits - 1))
    return [bits - 2] + list(range(bits - 2)) + [bits - 1]


def slot_of(distance, offsets):
    return sum(jnp.where(distance == offset, i, 0) for i, offset in enumerate(offsets))


def fetch_state(own, far, far_mask, entries, order, gate, late_gate, last_gate, group):
    count = lax.axis_size("req")
    size = own.shape[0]
    offsets, held = [0], [own]
    for step, bit in enumerate(order[:-1]):
        mask = 1 << bit
        moved = []
        for offset, value in zip(offsets, held):
            if offset == 0 and mask == far_mask:
                moved.append(far)
            else:
                moved.append(swap(after(value, *(late_gate if step else gate)), "req", mask))
        held = held + moved
        offsets = offsets + [offset ^ mask for offset in offsets]
    last = 1 << order[-1]
    every = jnp.arange(count, dtype=jnp.int32)
    bits = len(order)
    flipped = jnp.flip(entries.reshape((2,) * bits), bits - 1 - order[-1]).reshape(count)
    distance = entries ^ every
    source = jnp.where((distance & last) == 0, slot_of(distance, offsets), len(held))
    choices = jnp.stack([slot_of(flipped ^ every, offsets), source]).astype(jnp.int32)
    mine = lax.dynamic_slice_in_dim(choices, lax.axis_index("req"), 1, axis=1)[:, 0]
    begun = choose(after(mine[0:1], *last_gate), held, group, size)
    return mine[1], held + [swap(begun, "req", last)], begun


def norm_body(parts, group, local_groups, where_ref, *refs):
    y_refs = refs[:parts]
    gate_refs = refs[parts : 2 * parts]
    gain_refs = refs[2 * parts : 3 * parts]
    out_ref, done_ref, sem = refs[-3:]
    share, live = where_ref[0], where_ref[1]
    number, steps = pl.program_id(0), pl.num_programs(0)
    rows, width = y_refs[0].shape
    row_at = lax.broadcasted_iota(jnp.int32, (rows, 1), 0) + number * rows
    lanes = gain_refs[0].shape[1]
    chunks = width // lanes
    third = chunks * local_groups

    def placing(step, k):
        column = pl.multiple_of(((share ^ k) * local_groups + group) * width, width)
        at = pl.ds(pl.multiple_of(step * rows, rows), rows)
        return pltpu.make_async_copy(done_ref.at[step, k], out_ref.at[at, pl.ds(column, width)], sem.at[step, k])

    for k in range(parts):
        gate = gate_refs[k][...].astype(jnp.float32)
        gated = y_refs[k][...].astype(jnp.float32) * gate * (0.5 + 0.5 * jnp.tanh(0.5 * gate))
        mean_sq = jnp.mean(gated * gated, axis=1, keepdims=True)
        normed = gated * jnp.where(row_at < live, lax.rsqrt(mean_sq + 1e-05), 0.0)
        gains = gain_refs[k][...].astype(jnp.float32)
        first = group * chunks
        gain = sum(gains[first + i * third : first + i * third + chunks] for i in range(3))
        for chunk in range(chunks):
            cols = slice(chunk * lanes, (chunk + 1) * lanes)
            done_ref[number, k, :, cols] = (normed[:, cols] * gain[chunk : chunk + 1, :]).astype(jnp.bfloat16)
        placing(number, k).start()

    @pl.when(number == steps - 1)
    def _():
        for step in range(done_ref.shape[0]):
            for k in range(parts):
                placing(step, k).wait()


def norm_group(returned, gate, joined, where, group, local_groups, earlier):
    parts = joined.shape[0]
    rows, width = returned[0].shape[-2:]
    lanes, steps = 128, 2
    step = rows // steps
    specs = [pl.BlockSpec((step, width), lambda i, *_: (i, 0))] * parts
    specs += [
        pl.BlockSpec((step, width), functools.partial(lambda k, i, at: (i, (at[0] ^ k) * local_groups + group), k))
        for k in range(parts)
    ]
    specs += [
        pl.BlockSpec(
            (None, rows, lanes),
            functools.partial(lambda k, i, at: (at[0] ^ k, 0, joined.shape[2] // lanes - 1), k),
        )
        for k in range(parts)
    ]
    inputs = [where, *returned, *([gate] * parts), *([joined] * parts)]
    aliases = {}
    if earlier is not None:
        aliases = {len(inputs): 0}
        inputs.append(earlier)
        specs.append(pl.BlockSpec(memory_space=pl.ANY))
    return pl.pallas_call(
        functools.partial(norm_body, parts, group, local_groups),
        grid_spec=pltpu.PrefetchScalarGridSpec(
            num_scalar_prefetch=1,
            grid=(steps,),
            in_specs=specs,
            out_specs=pl.BlockSpec(memory_space=pl.ANY),
            scratch_shapes=[
                pltpu.VMEM((steps, parts, step, width), jnp.bfloat16),
                pltpu.SemaphoreType.DMA((steps, parts)),
            ],
        ),
        out_shape=jax.ShapeDtypeStruct(gate.shape, jnp.bfloat16),
        input_output_aliases=aliases,
        compiler_params=params(),
        cost_estimate=cost(3),
    )(*inputs)


def place_body(where_ref, in_ref, out_ref):
    parts, rows, width = in_ref.shape
    alive = lax.broadcasted_iota(jnp.int32, (rows, 1), 0) + pl.program_id(0) * rows < where_ref[1]
    for part in range(parts):
        value = in_ref[part].astype(jnp.float32)
        out_ref[:, part * width : (part + 1) * width] = jnp.where(alive, value, 0.0).astype(jnp.bfloat16)


def place_heads(returned, where):
    parts, rows, width = returned.shape
    step = rows // 2
    return pl.pallas_call(
        place_body,
        grid_spec=pltpu.PrefetchScalarGridSpec(
            num_scalar_prefetch=1,
            grid=(rows // step,),
            in_specs=[pl.BlockSpec((parts, step, width), lambda i, *_: (0, i, 0))],
            out_specs=pl.BlockSpec((step, parts * width), lambda i, *_: (i, 0)),
        ),
        out_shape=jax.ShapeDtypeStruct((rows, parts * width), jnp.bfloat16),
        compiler_params=params(),
        cost_estimate=cost(2),
    )(where, returned)


def per_device(
    ssm_input,
    ssm_gate,
    state_proj,
    step_raw,
    queries,
    fresh_kv,
    block_pool,
    state_pool,
    decay_log,
    step_bias,
    skip_gain,
    norm_gain,
    block_owner,
    block_slot,
    block_count,
    state_entry,
    suffix_len,
):
    request = lax.axis_index("req")
    share = lax.axis_index("tp")
    parts = lax.axis_size("tp")
    owners = lax.axis_size("req")
    rows = ssm_input.shape[1]
    groups = state_proj.shape[2] // (2 * STATE)
    local_groups = groups // parts
    group_width = ssm_input.shape[2] // groups
    head_total = step_raw.shape[2]
    heads = head_total // groups
    channels = group_width // heads
    q_width = queries.shape[2] // parts
    fresh_width = fresh_kv.shape[2] // parts
    pool_local = block_pool.shape[0]
    pool_total = pool_local * owners
    listed = min(block_owner.shape[1], pool_total)
    order = bit_order(owners, 0)
    first_bit = 1 << order[0]

    pieces = [
        (ssm_input[0], local_groups * group_width, lambda p: p),
        (state_proj[0], local_groups * 2 * STATE, lambda p: p),
        (queries[0], q_width, lambda p: p),
        (fresh_kv[0], fresh_width, lambda p: p),
        (step_raw[0], head_total, lambda p: 0),
    ]
    q_column = pieces[0][1] + pieces[1][1]
    step_column = q_column + q_width + fresh_width
    pool_own = jnp.transpose(block_pool, (0, 2, 1, 3))
    state_own = state_pool.reshape(local_groups * group_width, STATE)
    state_groups = [state_own[group * group_width : (group + 1) * group_width] for group in range(local_groups)]
    packed = pack(parts, pieces, after(norm_gain, pool_own).reshape(-1, 128))
    joined = spread(packed)

    far_mask = 1 << order[1]
    state_far = swap(state_own, "req", far_mask)
    pool_far = after(swap(pool_own, "req", first_bit), packed)
    pool_held = join(pool_own, pool_far)
    pools = [(pool_held, [0, first_bit])]
    for bit in [order[-1]] + order[1:-1]:
        mask = 1 << bit
        moved = []
        for index, (array, held) in enumerate(pools):
            gate = [state_far] if mask == far_mask and index > 0 else []
            moved.append((swap(after(array, *gate), "req", mask), [offset ^ mask for offset in held]))
        pools += moved

    entries = after(state_entry, pool_held)
    state_lists, begun = [None] * local_groups, []

    def fetch(group, last_gate):
        gates = ([pool_far], [array for array, _ in pools[1:3]]) if group % 2 == 0 else ([], [])
        source, values, sent = fetch_state(
            state_groups[group], state_far, far_mask, entries, bit_order(owners, group), *gates, last_gate, group
        )
        state_lists[group] = (source, values)
        begun.append(sent)

    for group in reversed(range(1, local_groups)):
        fetch(group, [])

    targets = after(block_owner, pool_held)[request] * pool_local + block_slot[request]
    often, place, total = block_places(targets, block_count[request], pool_total)
    where = jnp.stack([request, total]).astype(jnp.int32)
    live = jnp.stack([share, suffix_len[request] - share * rows]).astype(jnp.int32)

    where = after(where, *begun)
    mixed = attention(joined, pools, where, often, place, listed, q_column, q_width)
    attn_back = spread(mixed)
    fetch(0, [mixed])

    ssm_out = None
    skips = jnp.repeat(skip_gain, channels)[None, :]
    for group in reversed(range(local_groups)):
        mine = slice(group * heads, (group + 1) * heads)
        head_rows = jnp.zeros((8, head_total), jnp.float32)
        head_rows = head_rows.at[0, :heads].set(decay_log[mine])
        head_rows = head_rows.at[1, :heads].set(step_bias[mine])
        start = (share * local_groups + group) * heads
        shift = lax.rem(head_total - start, head_total)
        cols = slice(group * group_width, (group + 1) * group_width)
        source, values = state_lists[group]
        where = after(jnp.stack([share, shift, source]).astype(jnp.int32), mixed, begun[-1])
        scanned = scan_group(
            joined, step_column, values, where, head_rows, skips[:, cols], heads, group, local_groups
        )
        if group == 0:
            attn_out = place_heads(attn_back, after(live, scanned[0]))
            live = after(live, attn_out)
        ssm_out = norm_group(exchange(scanned), ssm_gate[0], joined, live, group, local_groups, ssm_out)
    return (ssm_out[None], attn_out[None])


def solution(mesh):
    return jax.shard_map(
        per_device,
        mesh=mesh,
        in_specs=(
            P("req", "tp", None),
            P("req", "tp", None),
            P("req", "tp", None),
            P("req", "tp", None),
            P("req", "tp", None),
            P("req", "tp", None),
            P("req", None, "tp", None),
            P("req", "tp", None, None),
            P("tp"),
            P("tp"),
            P("tp"),
            P("tp"),
            P(),
            P(),
            P(),
            P(),
            P(),
        ),
        out_specs=(P("req", "tp", None), P("req", "tp", None)),
        check_vma=False,
    )
```
